32 devices in a mesh: ctx: 8 (over y, x, core), tp: 4 (over z).
Axes of the slice: x: 2, y: 2, z: 4, core: 2. Of those that a mesh axis runs over, the one named last changes fastest.
Arguments:
- residual_in: bfloat16 [4096, 4096], P('ctx', 'tp'), may hold values from -6 to 6
- features: bfloat16 [3, 4096, 2048], P(None, 'ctx', 'tp'), may hold values from -6 to 6
- filter_taps: float32 [2048, 128], P('tp'), may hold values from -1.2 to 1.2
- filter_decay: float32 [2048], P('tp'), may hold values from 0.004 to 0.2
- skip_gain: float32 [2048], P('tp'), may hold values from -3 to 3
- out_weight: bfloat16 [2048, 4096], P('tp'), may hold values from -0.125 to 0.125
- norm_gain: float32 [4096], replicated, may hold values from 0.25 to 1.75
- qkv_weight: bfloat16 [3, 4096, 2048], P(None, None, 'tp'), may hold values from -1 to 1
- doc_lengths: int32 [8], replicated, may hold values from 1 to 3072, 4096 in all
Outputs:
- mixed_stream: bfloat16 [4096, 4096], P('ctx', 'tp')
- attended: bfloat16 [4096, 2048], P('ctx', 'tp')
The draws below stay inside these ranges and needn't reach their ends.
Inputs may be any that keep to these rules, and one draw needn't show every extreme that they name: doc_lengths sum to 4096; the longest document has exactly 3072 tokens.
All inputs are finite; a program needn't handle non-finite values.
Results may differ from the reference program's by a relative error of at most 0.0085.
Values may be sent and summed in bfloat16 or wider, within the bound.
A program may use at most 128 MiB of HBM per device.

```python
import math
import jax
import jax.numpy as jnp
import numpy as np
from jax import lax

D = 4096
HEADS = 16
HS = 128
HYENA_CH = 2048
TAPS = 128
DOCS = 8
TOKENS = 4096


def draw_residual_in(key, part):
    key = jax.random.fold_in(key, 1)
    jitter = jax.random.normal(key, (TOKENS, D), jnp.float32)
    drawn = jitter
    return jnp.clip(drawn, -6.0, 6.0).astype(jnp.bfloat16)


def draw_qkv_weight(key, part):
    key = jax.random.fold_in(key, 2)
    subkeys = jax.random.split(key, 1)
    weights = jnp.clip(jax.random.normal(subkeys[0], (3, D, HEADS * HS), jnp.float32), -6.0, 6.0) / math.sqrt(D)
    bound = 1.0 + 512 // D
    return jnp.clip(weights, -bound, bound).astype(jnp.bfloat16)


def shard_levels(own_key, dims, cuts, least, largest):
    factor_of, own = 1.0, jax.random.fold_in(own_key, 6)
    for axis_at, parts in cuts:
        heights = jnp.exp(jax.random.uniform(jax.random.fold_in(own, axis_at), (parts,), jnp.float32, least / len(cuts), largest / len(cuts)))
        factor_of = factor_of * jnp.repeat(heights, dims[axis_at] // parts).reshape([-1 if axis == axis_at else 1 for axis in range(len(dims))])
    return factor_of


def length_profile(count, total, limit, lean):
    portions = [(1 << 20) // math.isqrt(standing ** lean) + 1 for standing in range(2, count + 1)]
    surplus, counts = total - limit - (count - 1), [1] * (count - 1)
    while surplus > 0:
        movable = [i for i in range(count - 1) if counts[i] < limit]
        mass, left = sum([portions[i] for i in movable]), surplus
        for i in movable:
            more = min(limit - counts[i], max(1, left * portions[i] // mass), surplus)
            counts[i] = counts[i] + more
            surplus = surplus - more
    return np.array([limit] + counts)


def uneven_parts(rng, number_of, total, reach, lean):
    if number_of == 2:
        one = jax.random.randint(rng, (), max(1, total - reach), min(reach, total - 1) + 1)
        return jnp.stack([one, total - one])
    sizes = jnp.asarray(length_profile(number_of, total, reach, lean), jnp.int32)
    pairs = (number_of - 1) // 2
    source_of, receiver = sizes[1:1 + 2 * pairs:2], sizes[2:2 + 2 * pairs:2]
    margin = jnp.minimum(source_of - 1, reach - receiver)
    passed = jax.random.randint(jax.random.fold_in(rng, 1), (pairs,), 0, 1 << 20) % (margin + 1)
    sizes = sizes.at[1:1 + 2 * pairs:2].set(source_of - passed).at[2:2 + 2 * pairs:2].set(receiver + passed)
    return sizes[jax.random.permutation(jax.random.fold_in(rng, 2), number_of)]


def bell_draw(stream_key, dims, spread, most, shards=(), held_as=jnp.bfloat16):
    result = spread * jax.random.normal(stream_key, dims, jnp.float32)
    if shards:
        result = result * shard_levels(stream_key, dims, shards, -0.22, 0.18)
    return jnp.clip(result, -most, most).astype(held_as)


def setup_inputs(seed: int = 0) -> dict:
    streams_of = jax.random.split(jax.random.key(seed), 10)
    residual_in = draw_residual_in(jax.random.fold_in(streams_of[9], 71), 0)
    features = bell_draw(streams_of[1], (3, TOKENS, HYENA_CH), 1.0, 6.0, ((1, 8), (2, 4)))
    filter_taps = bell_draw(streams_of[2], (HYENA_CH, TAPS), 0.2, 1.2, ((0, 4),), jnp.float32)
    filter_decay = jnp.clip(jnp.exp(math.log(0.2) - 3.912023 * jax.random.uniform(streams_of[3], (HYENA_CH,), jnp.float32) ** shard_levels(streams_of[3], (HYENA_CH,), ((0, 4),), -0.2, 0.2)), 0.004, 0.2)
    skip_gain = bell_draw(streams_of[4], (HYENA_CH,), 1.0, 3.0, ((0, 4),), jnp.float32)
    out_weight = bell_draw(streams_of[5], (HYENA_CH, D), HYENA_CH ** -0.5, 0.125, ((0, 4),))
    norm_gain = jnp.clip(1.0 + 0.15 * jax.random.normal(streams_of[6], (D,), jnp.float32), 0.25, 1.75)
    qkv_weight = draw_qkv_weight(jax.random.fold_in(streams_of[9], 71), 0)
    doc_lengths = uneven_parts(streams_of[8], DOCS, TOKENS, 3 * TOKENS // 4, 2).astype(jnp.int32)
    return {"residual_in": residual_in, "features": features, "filter_taps": filter_taps, "filter_decay": filter_decay, "skip_gain": skip_gain, "out_weight": out_weight, "norm_gain": norm_gain, "qkv_weight": qkv_weight, "doc_lengths": doc_lengths}


eps = 1e-06
query_block = 512

def reference(residual_in, features, filter_taps, filter_decay, skip_gain, out_weight, norm_gain, qkv_weight, doc_lengths):
    query_h = features[0].astype(jnp.float32)
    mixed_in = features[1].astype(jnp.float32) * features[2].astype(jnp.float32)
    tap_index = jnp.arange(TAPS, dtype=jnp.float32)
    filt = filter_taps * jnp.exp(-filter_decay[:, None] * tap_index[None, :])
    padded = jnp.concatenate([jnp.zeros((TAPS - 1, HYENA_CH), mixed_in.dtype), mixed_in], axis=0)
    filt_t = filt.T

    def tap_fn(tap, acc):
        shifted = lax.dynamic_slice_in_dim(padded, (TAPS - 1 - tap).astype(jnp.int32), TOKENS, 0)
        coef = lax.dynamic_slice_in_dim(filt_t, tap.astype(jnp.int32), 1, 0)
        return acc + coef * shifted
    conv = lax.fori_loop(jnp.int32(0), jnp.int32(TAPS), tap_fn, jnp.zeros_like(mixed_in))
    gated = (query_h * (conv + skip_gain[None, :] * mixed_in)).astype(jnp.bfloat16)
    stream = residual_in.astype(jnp.float32) + jnp.dot(gated, out_weight, preferred_element_type=jnp.float32)
    mixed_stream = stream.astype(jnp.bfloat16)
    scale_rms = lax.rsqrt(lax.optimization_barrier(jnp.mean(stream * stream, axis=1, keepdims=True)) + eps)
    normed = (stream * scale_rms * norm_gain[None, :]).astype(jnp.bfloat16)
    query = jnp.dot(normed, qkv_weight[0], preferred_element_type=jnp.float32).astype(jnp.bfloat16)
    keys = jnp.dot(normed, qkv_weight[1], preferred_element_type=jnp.float32).astype(jnp.bfloat16)
    values = jnp.dot(normed, qkv_weight[2], preferred_element_type=jnp.float32).astype(jnp.bfloat16)
    ends = jnp.cumsum(doc_lengths).astype(jnp.int32)
    position = jnp.arange(TOKENS, dtype=jnp.int32)
    seg = lax.optimization_barrier(jnp.sum((ends[None, :] <= position[:, None]).astype(jnp.int32), axis=1)).astype(jnp.int32)
    scale = HS ** (-0.5)
    local_pos = jnp.arange(query_block, dtype=jnp.int32)

    def head_fn(head):
        q_head = lax.dynamic_slice_in_dim(query, head * HS, HS, 1)
        k_head = lax.dynamic_slice_in_dim(keys, head * HS, HS, 1)
        v_head = lax.dynamic_slice_in_dim(values, head * HS, HS, 1)

        def block_fn(block):
            first = (block * query_block).astype(jnp.int32)
            q_rows = lax.dynamic_slice_in_dim(q_head, first, query_block, 0)
            q_pos = first + local_pos
            q_seg = lax.dynamic_slice_in_dim(seg, first, query_block, 0)

            def tile(kb):
                k_first = (kb * query_block).astype(jnp.int32)
                k_rows = lax.dynamic_slice_in_dim(k_head, k_first, query_block, 0)
                k_pos = k_first + local_pos
                k_seg = lax.dynamic_slice_in_dim(seg, k_first, query_block, 0)
                scores = jnp.dot(q_rows, k_rows.T, preferred_element_type=jnp.float32) * scale
                allowed = (k_pos[None, :] <= q_pos[:, None]) & (k_seg[None, :] == q_seg[:, None])
                return (scores, allowed, k_first)

            def max_fn(kb, top):
                scores, allowed, unused = tile(kb)
                return jnp.maximum(top, lax.optimization_barrier(jnp.max(jnp.where(allowed, scores, -1e+30), axis=1, keepdims=True)))
            top = lax.fori_loop(jnp.int32(0), block.astype(jnp.int32) + 1, max_fn, jnp.full((query_block, 1), -1e+30, jnp.float32))

            def sum_fn(kb, carry):
                total, summed = carry
                scores, allowed, k_first = tile(kb)
                weights = jnp.where(allowed, jnp.exp(scores - top), 0.0)
                v_rows = lax.dynamic_slice_in_dim(v_head, k_first, query_block, 0)
                total = total + lax.optimization_barrier(jnp.sum(weights, axis=1, keepdims=True))
                summed = summed + jnp.dot(weights.astype(jnp.bfloat16), v_rows, preferred_element_type=jnp.float32)
                return (total, summed)
            total, summed = lax.fori_loop(jnp.int32(0), block.astype(jnp.int32) + 1, sum_fn, (jnp.zeros((query_block, 1), jnp.float32), jnp.zeros((query_block, HS), jnp.float32)))
            return summed / total
        blocks = lax.map(block_fn, jnp.arange(TOKENS // query_block, dtype=jnp.int32))
        return blocks.reshape(TOKENS, HS)
    heads_out = lax.map(head_fn, jnp.arange(HEADS, dtype=jnp.int32))
    attended = jnp.transpose(heads_out, (1, 0, 2)).reshape(TOKENS, HEADS * HS).astype(jnp.bfloat16)
    return (mixed_stream, attended)
```

```python
import functools
import jax
import jax.numpy as jnp
from jax import lax
from jax.experimental import pallas as pl
from jax.experimental.pallas import tpu as pltpu
from jax.sharding import PartitionSpec as P

D = 4096
HS = 128
LOG2E = 1.4426950408889634


eps = 1e-06


def flip(place, by):
    out = place
    bit = 1
    while bit <= by:
        if by & bit:
            out = out + bit - 2 * bit * ((place // bit) % 2)
        bit *= 2
    return out


def plane_kernel(devices, k_ref, v_ref, k_out, v_out, own_sem, send_sem, recv_sem, mate_send, mate_recv):
    me = lax.axis_index("ctx")
    chips = devices // 2
    rows = k_ref.shape[0]
    chip = me // 2
    core = me % 2
    mate = chip * 2 + 1 - core
    partners = [flip(chip, d) * 2 + core for d in range(1, chips)]

    barrier = pltpu.get_barrier_semaphore()
    for other in partners + [mate]:
        pl.semaphore_signal(barrier, inc=1, device_id={"ctx": other}, device_id_type=pl.DeviceIdType.MESH)
    pl.semaphore_wait(barrier, chips)

    outs = (k_out, v_out)
    ins = (k_ref, v_ref)

    def slot(b, place):
        return outs[b].at[pl.ds(pl.multiple_of(place * rows, rows), rows), :]

    def to_partner(b, d, src, place, target):
        return pltpu.make_async_remote_copy(
            src_ref=src, dst_ref=slot(b, place), send_sem=send_sem.at[b, d], recv_sem=recv_sem.at[b, d],
            device_id={"ctx": target}, device_id_type=pl.DeviceIdType.MESH)

    def to_mate(b, d, src, place):
        return pltpu.make_async_remote_copy(
            src_ref=src, dst_ref=slot(b, place), send_sem=mate_send.at[b, d], recv_sem=mate_recv.at[b, d],
            device_id={"ctx": mate}, device_id_type=pl.DeviceIdType.MESH)

    relayed = chips == 4
    direct = (1, 2) if relayed else tuple(range(1, chips))
    for b in range(2):
        for d in direct:
            to_partner(b, d, ins[b], me, partners[d - 1]).start()
        to_mate(b, 0, ins[b], me).start()
        pltpu.make_async_copy(ins[b], slot(b, me), own_sem.at[b]).start()
    for b in range(2):
        for d in direct:
            place = partners[d - 1]
            to_partner(b, d, slot(b, place), place, place).wait_recv()
            to_mate(b, d, slot(b, place), place).start()
            if relayed:

                @pl.when(core == d - 1)
                def _():
                    to_partner(b, 3, slot(b, place), place, partners[2 - d]).start()
    for b in range(2):
        if relayed:
            place = partners[2]
            to_partner(b, 3, slot(b, place), place, place).wait_recv()
            to_mate(b, 3, slot(b, place), place).start()
    for b in range(2):
        for d in range(1, chips):
            to_partner(b, d, ins[b], me, partners[d - 1]).wait_send()
        for d in range(chips):
            place = flip(chip, d) * 2 + 1 - core
            to_mate(b, d, slot(b, place), place).wait()
        pltpu.make_async_copy(ins[b], slot(b, me), own_sem.at[b]).wait()


def gather_plane(keys, values, devices):
    rows, cols = keys.shape
    chips = devices // 2
    full = jax.ShapeDtypeStruct((devices * rows, cols), keys.dtype)
    return pl.pallas_call(
        functools.partial(plane_kernel, devices),
        out_shape=(full, full),
        in_specs=[pl.BlockSpec(memory_space=pl.ANY)] * 2,
        out_specs=[pl.BlockSpec(memory_space=pl.ANY)] * 2,
        scratch_shapes=[
            pltpu.SemaphoreType.DMA((2,)),
            pltpu.SemaphoreType.DMA((2, chips)),
            pltpu.SemaphoreType.DMA((2, chips)),
            pltpu.SemaphoreType.DMA((2, chips)),
            pltpu.SemaphoreType.DMA((2, chips)),
        ],
        compiler_params=pltpu.CompilerParams(collective_id=1, has_side_effects=True),
        name="gather_keys_values",
    )(keys, values)


def attention_kernel(block, bounds, q_ref, k_ref, v_ref, low_ref, out_ref):
    rows = q_ref.shape[0]
    first = bounds[0]
    low = low_ref[...]
    q = q_ref[...]
    row = lax.broadcasted_iota(jnp.int32, (rows, block), 0) + first
    column = lax.broadcasted_iota(jnp.int32, (rows, block), 1)

    def step(at, carry):
        top, total, accum = carry
        start = pl.multiple_of(at * block, block)
        k = k_ref[pl.ds(start, block), :]
        v = v_ref[pl.ds(start, block), :]
        scores = lax.dot_general(q, k, (((1,), (1,)), ((), ())), preferred_element_type=jnp.float32)
        scores = scores * (HS ** (-0.5) * LOG2E)
        place = column + start
        allowed = (place <= row) & (place >= low)
        masked = jnp.where(allowed, scores, -1e30)
        new_top = jnp.maximum(top, jnp.max(masked, axis=1, keepdims=True))
        factor = jnp.exp2(top - new_top)
        weights = jnp.where(allowed, jnp.exp2(masked - new_top), 0.0)
        total = total * factor + jnp.sum(weights, axis=1, keepdims=True)
        accum = accum * factor + jnp.dot(weights.astype(jnp.bfloat16), v, preferred_element_type=jnp.float32)
        return new_top, total, accum

    init = (
        jnp.full((rows, 1), -1e30, jnp.float32),
        jnp.zeros((rows, 1), jnp.float32),
        jnp.zeros((rows, HS), jnp.float32),
    )
    top, total, accum = lax.fori_loop(bounds[1] // block, (first + rows) // block, step, init)
    out_ref[...] = (accum / total).astype(out_ref.dtype)


def attention(query, k_all, v_all, low, first):
    rows, cols = query.shape
    tokens = k_all.shape[0]
    heads = cols // HS
    bounds = jnp.stack([first, low[0]]).astype(jnp.int32)
    return pl.pallas_call(
        functools.partial(attention_kernel, rows),
        out_shape=jax.ShapeDtypeStruct((rows, cols), jnp.bfloat16),
        grid_spec=pltpu.PrefetchScalarGridSpec(
            num_scalar_prefetch=1,
            grid=(heads,),
            in_specs=[
                pl.BlockSpec((rows, HS), lambda h, b: (0, h)),
                pl.BlockSpec((tokens, HS), lambda h, b: (0, h)),
                pl.BlockSpec((tokens, HS), lambda h, b: (0, h)),
                pl.BlockSpec((rows, 1), lambda h, b: (0, 0)),
            ],
            out_specs=pl.BlockSpec((rows, HS), lambda h, b: (0, h)),
        ),
        compiler_params=pltpu.CompilerParams(vmem_limit_bytes=48 * 1024 * 1024),
        name="attention",
    )(bounds, query, k_all, v_all, low[:, None])


def shifted(value, axis, by):
    devices = lax.axis_size(axis)
    pairs = [(i, i + by) for i in range(devices) if 0 <= i + by < devices]
    return lax.ppermute(value, axis, pairs)


def body(
    residual_in,
    features,
    filter_taps,
    filter_decay,
    skip_gain,
    out_weight,
    norm_gain,
    qkv_weight,
    doc_lengths,
):
    rows = residual_in.shape[0]
    local_width = residual_in.shape[1]
    channels = filter_taps.shape[0]
    span = filter_taps.shape[1]
    query_h = features[0]
    key_h = features[1]
    value_h = features[2]
    edge_keys, edge_values = shifted(
        (key_h[rows - (span - 1) :], value_h[rows - (span - 1) :]), "ctx", 1
    )
    mixed_in = key_h.astype(jnp.float32) * value_h.astype(jnp.float32)
    before = edge_keys.astype(jnp.float32) * edge_values.astype(jnp.float32)
    extended = jnp.concatenate([before, mixed_in], axis=0)
    tap_index = jnp.arange(span, dtype=jnp.float32)
    filt = filter_taps * jnp.exp(-filter_decay[:, None] * tap_index[None, :])
    kernel = filt[:, ::-1].T[:, None, :]
    conv = lax.conv_general_dilated(
        extended[None],
        kernel,
        (1,),
        [(0, 0)],
        dimension_numbers=("NHC", "HIO", "NHC"),
        feature_group_count=channels,
        precision=lax.Precision.HIGHEST,
    )[0]
    gated = (query_h.astype(jnp.float32) * (conv + skip_gain[None, :] * mixed_in)).astype(
        jnp.bfloat16
    )
    offset = lax.axis_index("tp") * local_width
    gain_local = lax.dynamic_slice_in_dim(norm_gain, offset, local_width, 0)
    parts = lax.axis_size("ctx")
    planes = lax.axis_size("tp")
    share = channels // parts
    mine = lax.dynamic_slice_in_dim(out_weight, lax.axis_index("ctx") * share, share, 0)
    moved = lax.all_to_all(mine, "tp", split_axis=1, concat_axis=0, tiled=True)
    columns = lax.all_gather(moved, "ctx", axis=0, tiled=False)
    columns = columns.reshape(parts, planes, share, local_width).transpose(1, 0, 2, 3)
    columns = columns.reshape(planes * channels, local_width)
    gated_all = lax.all_gather(gated, "tp", axis=1, tiled=True)
    stream = residual_in.astype(jnp.float32) + jnp.dot(gated_all, columns, preferred_element_type=jnp.float32)
    mixed_stream = stream.astype(jnp.bfloat16)
    scaled = (stream * gain_local[None, :]).astype(jnp.bfloat16)
    squares = lax.psum(jnp.sum(stream * stream, axis=1), "tp")
    scale_rms = lax.rsqrt(squares / D + eps)
    piece = lax.all_gather(scaled, "tp", axis=1, tiled=True)

    def project(weight):
        product = jnp.dot(piece, weight, preferred_element_type=jnp.float32)
        return (product * scale_rms[:, None]).astype(jnp.bfloat16)

    query = project(qkv_weight[0])
    keys = project(qkv_weight[1])
    values = project(qkv_weight[2])
    ends = jnp.cumsum(doc_lengths)
    first = lax.axis_index("ctx") * rows
    q_pos = first + jnp.arange(rows, dtype=jnp.int32)
    low = jnp.max(jnp.where(ends[None, :] <= q_pos[:, None], ends[None, :], 0), axis=1).astype(jnp.int32)
    k_all, v_all = gather_plane(keys, values, parts)
    attended = attention(query, k_all, v_all, low, first)
    return (mixed_stream, attended)


def solution(mesh):
    return jax.shard_map(
        body,
        mesh=mesh,
        in_specs=(
            P("ctx", "tp"),
            P(None, "ctx", "tp"),
            P("tp", None),
            P("tp"),
            P("tp"),
            P("tp", None),
            P(),
            P(None, None, "tp"),
            P(),
        ),
        out_specs=(P("ctx", "tp"), P("ctx", "tp")),
        check_vma=False,
    )
```

```python
import functools
import jax
import jax.numpy as jnp
from jax import lax
from jax.experimental import pallas as pl
from jax.experimental.pallas import tpu as pltpu
from jax.sharding import PartitionSpec as P

D = 4096
HS = 128
LOG2E = 1.4426950408889634


eps = 1e-06


def flip(place, by):
    out = place
    bit = 1
    while bit <= by:
        if by & bit:
            out = out + bit - 2 * bit * ((place // bit) % 2)
        bit *= 2
    return out


def send(src, dst, sent, landed, device):
    return pltpu.make_async_remote_copy(
        src_ref=src, dst_ref=dst, send_sem=sent, recv_sem=landed,
        device_id=device, device_id_type=pl.DeviceIdType.MESH)


def greet(others):
    barrier = pltpu.get_barrier_semaphore()
    for other in others:
        pl.semaphore_signal(barrier, inc=1, device_id=other, device_id_type=pl.DeviceIdType.MESH)
    pl.semaphore_wait(barrier, len(others))


def deal_kernel(devices, planes, g_ref, w_ref, g_out, w_out, own_sem, g_send, g_recv, z_send, z_recv, p_send, p_recv, m_send, m_recv):
    me = lax.axis_index("ctx")
    z = lax.axis_index("tp")
    chips = devices // 2
    tokens, wide = g_ref.shape
    depth = w_ref.shape[0]
    width = w_out.shape[1]
    rows, half = depth // chips, width // 2
    chip = me // 2
    core = me % 2
    mate = chip * 2 + 1 - core
    partners = [flip(chip, d) * 2 + core for d in range(1, chips)]
    others = [(z + s) % planes for s in range(1, planes)]
    greet([{"ctx": p} for p in partners] + [{"ctx": mate}] + [{"tp": t} for t in others])

    def slot(origin, from_chip, from_core):
        return w_out.at[
            pl.ds(pl.multiple_of(origin * depth + from_chip * rows, rows), rows),
            pl.ds(pl.multiple_of(from_core * half, half), half)]

    def g_slot(origin):
        return g_out.at[:, pl.ds(pl.multiple_of(origin * wide, wide), wide)]

    def to_plane(target):
        src = w_ref.at[
            pl.ds(pl.multiple_of(chip * rows, rows), rows),
            pl.ds(pl.multiple_of(target * width + core * half, half), half)]
        return send(src, slot(z, chip, core), z_send.at[target], z_recv.at[z], {"tp": target})

    def from_plane(origin):
        place = slot(origin, chip, core)
        return send(place, place, z_send.at[origin], z_recv.at[origin], {"tp": origin})

    def to_partner(s, d, from_chip, target):
        place = slot(others[s], from_chip, core)
        return send(place, place, p_send.at[s, d], p_recv.at[s, d], {"ctx": target})

    def to_mate(s, d, from_core):
        place = slot(others[s], flip(chip, d), from_core)
        return send(place, place, m_send.at[s, d], m_recv.at[s, d], {"ctx": mate})

    def hop(origin, sent, target):
        place = g_slot(origin)
        return send(place, place, g_send.at[sent], g_recv.at[origin], {"tp": target})

    def first_hop(sent, target):
        return send(g_ref, g_slot(z), g_send.at[sent], g_recv.at[z], {"tp": target})

    for s in range(planes - 1):
        to_plane(others[s]).start()

    @pl.when(z + 1 < planes)
    def _():
        first_hop(planes, z + 1).start()

    @pl.when(z > 0)
    def _():
        first_hop(planes + 1, z - 1).start()

    own = pltpu.make_async_copy(g_ref, g_slot(z), own_sem.at[0])
    own.start()
    kept = pltpu.make_async_copy(
        w_ref.at[:, pl.ds(pl.multiple_of(z * width, width), width)],
        w_out.at[pl.ds(pl.multiple_of(z * depth, depth), depth), :], own_sem.at[1])
    kept.start()

    def relay(s):
        @pl.when(z - s >= 0)
        def _():
            hop(z - s, z - s, z).wait_recv()

            @pl.when(z + 1 < planes)
            def _():
                hop(z - s, z - s, z + 1).start()

        @pl.when(z + s < planes)
        def _():
            hop(z + s, z + s, z).wait_recv()

            @pl.when(z > 0)
            def _():
                hop(z + s, z + s, z - 1).start()

    relayed = chips == 4
    direct = (1, 2) if relayed else tuple(range(1, chips))
    for s in range(planes - 1):
        from_plane(others[s]).wait_recv()
        for d in direct:
            to_partner(s, d, chip, partners[d - 1]).start()
        to_mate(s, 0, core).start()
    relay(1)
    for s in range(planes - 1):
        for d in direct:
            to_partner(s, d, flip(chip, d), partners[d - 1]).wait_recv()
            to_mate(s, d, core).start()
            if relayed:

                @pl.when(core == d - 1)
                def _():
                    to_partner(s, 3, flip(chip, d), partners[2 - d]).start()
    for s in range(2, planes):
        relay(s)
    for s in range(planes - 1):
        if relayed:
            to_partner(s, 3, flip(chip, 3), partners[2]).wait_recv()
            to_mate(s, 3, core).start()
    for s in range(planes - 1):
        to_plane(others[s]).wait_send()
        for d in range(1, chips):
            to_partner(s, d, flip(chip, d), partners[d - 1]).wait_send()
        for d in range(chips):
            to_mate(s, d, core).wait_send()
            to_mate(s, d, 1 - core).wait_recv()

    @pl.when(z + 1 < planes)
    def _():
        first_hop(planes, z + 1).wait_send()

    @pl.when(z > 0)
    def _():
        first_hop(planes + 1, z - 1).wait_send()

    for s in range(1, planes):

        @pl.when((z - s >= 0) & (z + 1 < planes))
        def _():
            hop(z - s, z - s, z + 1).wait_send()

        @pl.when((z + s < planes) & (z > 0))
        def _():
            hop(z + s, z + s, z - 1).wait_send()

    own.wait()
    kept.wait()


def deal(gated, out_weight, devices, planes):
    tokens, wide = gated.shape
    depth, full = out_weight.shape
    chips = devices // 2
    dma = pltpu.SemaphoreType.DMA
    return pl.pallas_call(
        functools.partial(deal_kernel, devices, planes),
        out_shape=(
            jax.ShapeDtypeStruct((tokens, planes * wide), gated.dtype),
            jax.ShapeDtypeStruct((planes * depth, full // planes), out_weight.dtype),
        ),
        in_specs=[pl.BlockSpec(memory_space=pl.ANY)] * 2,
        out_specs=[pl.BlockSpec(memory_space=pl.ANY)] * 2,
        scratch_shapes=[
            dma((2,)), dma((planes + 2,)), dma((planes,)), dma((planes,)), dma((planes,)),
            dma((planes - 1, chips)), dma((planes - 1, chips)), dma((planes - 1, chips)), dma((planes - 1, chips)),
        ],
        compiler_params=pltpu.CompilerParams(collective_id=2, has_side_effects=True),
        name="deal_gated_and_columns",
    )(gated, out_weight)


def attention_kernel(devices, q_ref, k_ref, v_ref, low_ref, out_ref, k_all, v_all, top_ref, total_ref, accum_ref,
                     own_sem, send_sem, recv_sem, mate_send, mate_recv):
    me = lax.axis_index("ctx")
    chips = devices // 2
    rows, cols = q_ref.shape
    chip = me // 2
    core = me % 2
    mate = chip * 2 + 1 - core
    partners = [flip(chip, d) * 2 + core for d in range(1, chips)]
    greet([{"ctx": p} for p in partners] + [{"ctx": mate}])
    outs = (k_all, v_all)
    ins = (k_ref, v_ref)

    def slot(b, place):
        return outs[b].at[pl.ds(pl.multiple_of(place * rows, rows), rows), :]

    def to_partner(b, d, src, place, target):
        return send(src, slot(b, place), send_sem.at[b, d], recv_sem.at[b, d], {"ctx": target})

    def to_mate(b, d, src, place):
        return send(src, slot(b, place), mate_send.at[b, d], mate_recv.at[b, d], {"ctx": mate})

    pair = min(2 * HS, cols)
    pairs = cols // pair

    def attend(place, at):
        start = pl.multiple_of(place * rows, rows)
        row = lax.broadcasted_iota(jnp.int32, (rows, rows), 0) + me * rows
        column = lax.broadcasted_iota(jnp.int32, (rows, rows), 1) + start
        allowed = (column <= row) & (column >= low_ref[...])
        for inner in range(pair // HS):
            lanes = pl.ds(pl.multiple_of(at * pair + inner * HS, HS), HS)
            head = at * (pair // HS) + inner
            scores = lax.dot_general(
                q_ref[:, lanes], k_all[pl.ds(start, rows), lanes], (((1,), (1,)), ((), ())),
                preferred_element_type=jnp.float32)
            masked = jnp.where(allowed, scores * (HS ** (-0.5) * LOG2E), -1e30)
            top = top_ref[head]
            new_top = jnp.maximum(top, jnp.max(masked, axis=1, keepdims=True))
            factor = jnp.exp2(top - new_top)
            weights = jnp.exp2(masked - new_top)
            total_ref[head] = total_ref[head] * factor + jnp.sum(weights, axis=1, keepdims=True)
            accum_ref[:, lanes] = accum_ref[:, lanes] * factor + jnp.dot(
                weights.astype(jnp.bfloat16), v_all[pl.ds(start, rows), lanes], preferred_element_type=jnp.float32)
            top_ref[head] = new_top

    def attend_chip(from_chip, first_core):
        def step(i, unused):
            place = from_chip * 2 + (first_core + i // pairs) % 2

            @pl.when(place <= me)
            def _():
                attend(place, i % pairs)

            return unused

        lax.fori_loop(0, 2 * pairs, step, 0)

    for b in range(2):
        for d in ((1, 2) if chips == 4 else tuple(range(1, chips))):
            to_partner(b, d, ins[b], me, partners[d - 1]).start()
        to_mate(b, 0, ins[b], me).start()
        pltpu.make_async_copy(ins[b], slot(b, me), own_sem.at[b]).start()
    top_ref[...] = jnp.full(top_ref.shape, -1e20, jnp.float32)
    total_ref[...] = jnp.zeros(total_ref.shape, jnp.float32)
    accum_ref[...] = jnp.zeros(accum_ref.shape, jnp.float32)

    def mate_landed(d):
        for b in range(2):
            place = flip(chip, d) * 2 + 1 - core
            to_mate(b, d, slot(b, place), place).wait_recv()

    def partner_landed(d):
        for b in range(2):
            place = partners[d - 1]
            to_partner(b, d, slot(b, place), place, place).wait_recv()
            to_mate(b, d, slot(b, place), place).start()
            if chips == 4 and d < 3:

                @pl.when(core == d - 1)
                def _():
                    to_partner(b, 3, slot(b, place), place, partners[2 - d]).start()

    for b in range(2):
        pltpu.make_async_copy(ins[b], slot(b, me), own_sem.at[b]).wait()
    mate_landed(0)
    attend_chip(chip, core)
    if chips == 4:
        for d in (1, 2):
            partner_landed(d)
        for d in (1, 2):
            mate_landed(d)

        def both(d, unused):
            from_chip = (1 - d) * flip(chip, 1) + d * flip(chip, 2)
            attend_chip(from_chip, 0)
            return unused

        lax.fori_loop(0, 2, both, 0)
        partner_landed(3)
        mate_landed(3)
        attend_chip(flip(chip, 3), 0)
    else:
        for d in range(1, chips):
            partner_landed(d)
        for d in range(1, chips):
            mate_landed(d)

        def later(d, unused):
            attend_chip((chip + d) % chips, 0)
            return unused

        lax.fori_loop(1, chips, later, 0)
    for head in range(cols // HS):
        lanes = pl.ds(head * HS, HS)
        out_ref[:, lanes] = (accum_ref[:, lanes] / total_ref[head]).astype(out_ref.dtype)
    for b in range(2):
        for d in range(1, chips):
            to_partner(b, d, ins[b], me, partners[d - 1]).wait_send()
        for d in range(chips):
            to_mate(b, d, ins[b], me).wait_send()


def attention(query, keys, values, low, devices):
    rows, cols = query.shape
    chips = devices // 2
    dma = pltpu.SemaphoreType.DMA
    return pl.pallas_call(
        functools.partial(attention_kernel, devices),
        out_shape=jax.ShapeDtypeStruct((rows, cols), jnp.bfloat16),
        in_specs=[pl.BlockSpec(memory_space=pltpu.VMEM)] * 4,
        out_specs=pl.BlockSpec(memory_space=pltpu.VMEM),
        scratch_shapes=[
            pltpu.VMEM((devices * rows, cols), jnp.bfloat16),
            pltpu.VMEM((devices * rows, cols), jnp.bfloat16),
            pltpu.VMEM((cols // HS, rows, 1), jnp.float32),
            pltpu.VMEM((cols // HS, rows, 1), jnp.float32),
            pltpu.VMEM((rows, cols), jnp.float32),
            dma((2,)), dma((2, chips)), dma((2, chips)), dma((2, chips)), dma((2, chips)),
        ],
        compiler_params=pltpu.CompilerParams(
            collective_id=1, has_side_effects=True, vmem_limit_bytes=48 * 1024 * 1024),
        name="attention",
    )(query, keys, values, low[:, None])


def shifted(value, axis, by):
    devices = lax.axis_size(axis)
    pairs = [(i, i + by) for i in range(devices) if 0 <= i + by < devices]
    return lax.ppermute(value, axis, pairs)


def body(
    residual_in,
    features,
    filter_taps,
    filter_decay,
    skip_gain,
    out_weight,
    norm_gain,
    qkv_weight,
    doc_lengths,
):
    rows = residual_in.shape[0]
    local_width = residual_in.shape[1]
    channels = filter_taps.shape[0]
    span = filter_taps.shape[1]
    query_h = features[0]
    key_h = features[1]
    value_h = features[2]
    edge_keys, edge_values = shifted(
        (key_h[rows - (span - 1) :], value_h[rows - (span - 1) :]), "ctx", 1
    )
    mixed_in = key_h.astype(jnp.float32) * value_h.astype(jnp.float32)
    before = edge_keys.astype(jnp.float32) * edge_values.astype(jnp.float32)
    extended = jnp.concatenate([before, mixed_in], axis=0)
    tap_index = jnp.arange(span, dtype=jnp.float32)
    filt = filter_taps * jnp.exp(-filter_decay[:, None] * tap_index[None, :])
    kernel = filt[:, ::-1].T[:, None, :]
    conv = lax.conv_general_dilated(
        extended[None],
        kernel,
        (1,),
        [(0, 0)],
        dimension_numbers=("NHC", "HIO", "NHC"),
        feature_group_count=channels,
        precision=lax.Precision.HIGHEST,
    )[0]
    gated = (query_h.astype(jnp.float32) * (conv + skip_gain[None, :] * mixed_in)).astype(
        jnp.bfloat16
    )
    offset = lax.axis_index("tp") * local_width
    gain_local = lax.dynamic_slice_in_dim(norm_gain, offset, local_width, 0)
    parts = lax.axis_size("ctx")
    gated_all, columns = deal(gated, out_weight, parts, lax.axis_size("tp"))
    stream = residual_in.astype(jnp.float32) + jnp.dot(gated_all, columns, preferred_element_type=jnp.float32)
    mixed_stream = stream.astype(jnp.bfloat16)
    scaled = (stream * gain_local[None, :]).astype(jnp.bfloat16)
    squares = lax.psum(jnp.sum(stream * stream, axis=1), "tp")
    scale_rms = lax.rsqrt(squares / D + eps)
    piece = lax.all_gather(scaled, "tp", axis=1, tiled=True)

    def project(weight):
        product = jnp.dot(piece, weight, preferred_element_type=jnp.float32)
        return (product * scale_rms[:, None]).astype(jnp.bfloat16)

    query = project(qkv_weight[0])
    keys = project(qkv_weight[1])
    values = project(qkv_weight[2])
    ends = jnp.cumsum(doc_lengths)
    first = lax.axis_index("ctx") * rows
    q_pos = first + jnp.arange(rows, dtype=jnp.int32)
    low = jnp.max(jnp.where(ends[None, :] <= q_pos[:, None], ends[None, :], 0), axis=1).astype(jnp.int32)
    attended = attention(query, keys, values, low, parts)
    return (mixed_stream, attended)


def solution(mesh):
    return jax.shard_map(
        body,
        mesh=mesh,
        in_specs=(
            P("ctx", "tp"),
            P(None, "ctx", "tp"),
            P("tp", None),
            P("tp"),
            P("tp"),
            P("tp", None),
            P(),
            P(None, None, "tp"),
            P(),
        ),
        out_specs=(P("ctx", "tp"), P("ctx", "tp")),
        check_vma=False,
    )
```

```python
import functools
import jax
import jax.numpy as jnp
from jax import lax
from jax.experimental import pallas as pl
from jax.experimental.pallas import tpu as pltpu
from jax.sharding import PartitionSpec as P

D = 4096
HS = 128
LOG2E = 1.4426950408889634


eps = 1e-06


def flip(place, by):
    out = place
    bit = 1
    while bit <= by:
        if by & bit:
            out = out + bit - 2 * bit * ((place // bit) % 2)
        bit *= 2
    return out


def send(src, dst, sent, landed, device):
    return pltpu.make_async_remote_copy(
        src_ref=src, dst_ref=dst, send_sem=sent, recv_sem=landed,
        device_id=device, device_id_type=pl.DeviceIdType.MESH)


def greet(others):
    barrier = pltpu.get_barrier_semaphore()
    for other in others:
        pl.semaphore_signal(barrier, inc=1, device_id=other, device_id_type=pl.DeviceIdType.MESH)
    pl.semaphore_wait(barrier, len(others))


def deal_kernel(devices, planes, g_ref, w_ref, g_out, w_out, own_sem, g_send, g_recv, z_send, z_recv, p_send, p_recv, m_send, m_recv):
    me = lax.axis_index("ctx")
    z = lax.axis_index("tp")
    chips = devices // 2
    tokens, wide = g_ref.shape
    depth = w_ref.shape[0]
    width = w_out.shape[1]
    rows, half = depth // chips, width // 2
    chip = me // 2
    core = me % 2
    mate = chip * 2 + 1 - core
    partners = [flip(chip, d) * 2 + core for d in range(1, chips)]
    others = [(z + s) % planes for s in range(1, planes)]
    greet([{"ctx": p} for p in partners] + [{"ctx": mate}] + [{"tp": t} for t in others])

    def slot(origin, from_chip, from_core):
        return w_out.at[
            pl.ds(pl.multiple_of(origin * depth + from_chip * rows, rows), rows),
            pl.ds(pl.multiple_of(from_core * half, half), half)]

    def g_slot(origin):
        return g_out.at[:, pl.ds(pl.multiple_of(origin * wide, wide), wide)]

    def to_plane(target):
        src = w_ref.at[
            pl.ds(pl.multiple_of(chip * rows, rows), rows),
            pl.ds(pl.multiple_of(target * width + core * half, half), half)]
        return send(src, slot(z, chip, core), z_send.at[target], z_recv.at[z], {"tp": target})

    def from_plane(origin):
        place = slot(origin, chip, core)
        return send(place, place, z_send.at[origin], z_recv.at[origin], {"tp": origin})

    def to_partner(s, d, from_chip, target):
        place = slot(others[s], from_chip, core)
        return send(place, place, p_send.at[s, d], p_recv.at[s, d], {"ctx": target})

    def to_mate(s, d, from_core):
        place = slot(others[s], flip(chip, d), from_core)
        return send(place, place, m_send.at[s, d], m_recv.at[s, d], {"ctx": mate})

    def hop(origin, sent, target):
        place = g_slot(origin)
        return send(place, place, g_send.at[sent], g_recv.at[origin], {"tp": target})

    def first_hop(sent, target):
        return send(g_ref, g_slot(z), g_send.at[sent], g_recv.at[z], {"tp": target})

    for s in range(planes - 1):
        to_plane(others[s]).start()

    @pl.when(z + 1 < planes)
    def _():
        first_hop(planes, z + 1).start()

    @pl.when(z > 0)
    def _():
        first_hop(planes + 1, z - 1).start()

    own = pltpu.make_async_copy(g_ref, g_slot(z), own_sem.at[0])
    own.start()
    kept = pltpu.make_async_copy(
        w_ref.at[:, pl.ds(pl.multiple_of(z * width, width), width)],
        w_out.at[pl.ds(pl.multiple_of(z * depth, depth), depth), :], own_sem.at[1])
    kept.start()

    def relay(s):
        @pl.when(z - s >= 0)
        def _():
            hop(z - s, z - s, z).wait_recv()

            @pl.when(z + 1 < planes)
            def _():
                hop(z - s, z - s, z + 1).start()

        @pl.when(z + s < planes)
        def _():
            hop(z + s, z + s, z).wait_recv()

            @pl.when(z > 0)
            def _():
                hop(z + s, z + s, z - 1).start()

    relayed = chips == 4
    direct = (1, 2) if relayed else tuple(range(1, chips))
    for s in range(planes - 1):
        from_plane(others[s]).wait_recv()
        for d in direct:
            to_partner(s, d, chip, partners[d - 1]).start()
        to_mate(s, 0, core).start()
    relay(1)
    for s in range(planes - 1):
        for d in direct:
            to_partner(s, d, flip(chip, d), partners[d - 1]).wait_recv()
            to_mate(s, d, core).start()
            if relayed:

                @pl.when(core == d - 1)
                def _():
                    to_partner(s, 3, flip(chip, d), partners[2 - d]).start()
    for s in range(2, planes):
        relay(s)
    for s in range(planes - 1):
        if relayed:
            to_partner(s, 3, flip(chip, 3), partners[2]).wait_recv()
            to_mate(s, 3, core).start()
    for s in range(planes - 1):
        to_plane(others[s]).wait_send()
        for d in range(1, chips):
            to_partner(s, d, flip(chip, d), partners[d - 1]).wait_send()
        for d in range(chips):
            to_mate(s, d, core).wait_send()
            to_mate(s, d, 1 - core).wait_recv()

    @pl.when(z + 1 < planes)
    def _():
        first_hop(planes, z + 1).wait_send()

    @pl.when(z > 0)
    def _():
        first_hop(planes + 1, z - 1).wait_send()

    for s in range(1, planes):

        @pl.when((z - s >= 0) & (z + 1 < planes))
        def _():
            hop(z - s, z - s, z + 1).wait_send()

        @pl.when((z + s < planes) & (z > 0))
        def _():
            hop(z + s, z + s, z - 1).wait_send()

    own.wait()
    kept.wait()


def deal(gated, out_weight, devices, planes):
    tokens, wide = gated.shape
    depth, full = out_weight.shape
    chips = devices // 2
    dma = pltpu.SemaphoreType.DMA
    return pl.pallas_call(
        functools.partial(deal_kernel, devices, planes),
        out_shape=(
            jax.ShapeDtypeStruct((tokens, planes * wide), gated.dtype),
            jax.ShapeDtypeStruct((planes * depth, full // planes), out_weight.dtype),
        ),
        in_specs=[pl.BlockSpec(memory_space=pl.ANY)] * 2,
        out_specs=[pl.BlockSpec(memory_space=pl.ANY)] * 2,
        scratch_shapes=[
            dma((2,)), dma((planes + 2,)), dma((planes,)), dma((planes,)), dma((planes,)),
            dma((planes - 1, chips)), dma((planes - 1, chips)), dma((planes - 1, chips)), dma((planes - 1, chips)),
        ],
        compiler_params=pltpu.CompilerParams(collective_id=2, has_side_effects=True),
        name="deal_gated_and_columns",
    )(gated, out_weight)


def attention_kernel(devices, q_ref, k_ref, v_ref, low_ref, out_ref, k_all, v_all, top_ref, total_ref, accum_ref,
                     own_sem, send_sem, recv_sem, mate_send, mate_recv):
    me = lax.axis_index("ctx")
    chips = devices // 2
    rows, cols = q_ref.shape
    chip = me // 2
    core = me % 2
    mate = chip * 2 + 1 - core
    partners = [flip(chip, d) * 2 + core for d in range(1, chips)]
    greet([{"ctx": p} for p in partners] + [{"ctx": mate}])
    outs = (k_all, v_all)
    ins = (k_ref, v_ref)
    part = rows // 2
    heads = cols // HS

    def slot(b, place):
        return outs[b % 2].at[pl.ds(pl.multiple_of(place * rows + (b // 2) * part, part), part), :]

    def source(b):
        return ins[b % 2].at[pl.ds((b // 2) * part, part), :]

    def to_partner(b, d, src, place, target):
        return send(src, slot(b, place), send_sem.at[b, d], recv_sem.at[b, d], {"ctx": target})

    def to_mate(b, d, src, place):
        return send(src, slot(b, place), mate_send.at[b, d], mate_recv.at[b, d], {"ctx": mate})

    def attend(place, side, causal):
        start = pl.multiple_of(place * rows + side * part, part)
        column = lax.broadcasted_iota(jnp.int32, (rows, part), 1) + start
        allowed = column >= low_ref[...]
        if causal:
            row = lax.broadcasted_iota(jnp.int32, (rows, part), 0) + me * rows
            allowed = allowed & (column <= row)
        lanes = [pl.ds(h * HS, HS) for h in range(heads)]
        tops = [top_ref[h] for h in range(heads)]
        totals = [total_ref[h] for h in range(heads)]
        sums = [accum_ref[:, lanes[h]] for h in range(heads)]
        for h in range(heads):
            scores = lax.dot_general(
                q_ref[:, lanes[h]], k_all[pl.ds(start, part), lanes[h]], (((1,), (1,)), ((), ())),
                preferred_element_type=jnp.float32)
            masked = jnp.where(allowed, scores * (HS ** (-0.5) * LOG2E), -1e30)
            new_top = jnp.maximum(tops[h], jnp.max(masked, axis=1, keepdims=True))
            factor = jnp.exp2(tops[h] - new_top)
            weights = jnp.exp2(masked - new_top)
            totals[h] = totals[h] * factor + jnp.sum(weights, axis=1, keepdims=True)
            sums[h] = sums[h] * factor + jnp.dot(
                weights.astype(jnp.bfloat16), v_all[pl.ds(start, part), lanes[h]],
                preferred_element_type=jnp.float32)
            tops[h] = new_top
        for h in range(heads):
            top_ref[h] = tops[h]
            total_ref[h] = totals[h]
            accum_ref[:, lanes[h]] = sums[h]

    def attend_earlier(place, side):
        @pl.when(place < me)
        def _():
            attend(place, side, False)

    for b in range(4):
        for d in ((1, 2) if chips == 4 else tuple(range(1, chips))):
            to_partner(b, d, source(b), me, partners[d - 1]).start()
        to_mate(b, 0, source(b), me).start()
        pltpu.make_async_copy(source(b), slot(b, me), own_sem.at[b]).start()
    top_ref[...] = jnp.full(top_ref.shape, -1e20, jnp.float32)
    total_ref[...] = jnp.zeros(total_ref.shape, jnp.float32)
    accum_ref[...] = jnp.zeros(accum_ref.shape, jnp.float32)

    def mate_landed(d, side):
        for b in (2 * side, 2 * side + 1):
            place = flip(chip, d) * 2 + 1 - core
            to_mate(b, d, slot(b, place), place).wait_recv()

    def partner_landed(d, side):
        for b in (2 * side, 2 * side + 1):
            place = partners[d - 1]
            to_partner(b, d, slot(b, place), place, place).wait_recv()
            to_mate(b, d, slot(b, place), place).start()
            if chips == 4 and d < 3:

                @pl.when(core == d - 1)
                def _():
                    to_partner(b, 3, slot(b, place), place, partners[2 - d]).start()

    for b in range(4):
        pltpu.make_async_copy(source(b), slot(b, me), own_sem.at[b]).wait()

    def own(side, unused):
        attend(me, side, True)
        return unused

    lax.fori_loop(0, 2, own, 0)
    for side in range(2):
        mate_landed(0, side)

    def beside(side, unused):
        attend_earlier(mate, side)
        return unused

    lax.fori_loop(0, 2, beside, 0)
    if chips == 4:
        for side in range(2):
            for d in (1, 2):
                partner_landed(d, side)
            for d in (1, 2):
                mate_landed(d, side)

            def near(i, unused):
                from_chip = (1 - i // 2) * flip(chip, 1) + (i // 2) * flip(chip, 2)
                attend_earlier(from_chip * 2 + i % 2, side)
                return unused

            lax.fori_loop(0, 4, near, 0)
        for side in range(2):
            partner_landed(3, side)
            mate_landed(3, side)

            def far(i, unused):
                attend_earlier(flip(chip, 3) * 2 + i, side)
                return unused

            lax.fori_loop(0, 2, far, 0)
    else:
        for side in range(2):
            for d in range(1, chips):
                partner_landed(d, side)
            for d in range(1, chips):
                mate_landed(d, side)

            def later(i, unused):
                attend_earlier(((chip + i // 2) % chips) * 2 + i % 2, side)
                return unused

            lax.fori_loop(2, 2 * chips, later, 0)
    for h in range(heads):
        lanes = pl.ds(h * HS, HS)
        out_ref[:, lanes] = (accum_ref[:, lanes] / total_ref[h]).astype(out_ref.dtype)
    for b in range(4):
        for d in range(1, chips):
            to_partner(b, d, source(b), me, partners[d - 1]).wait_send()
        for d in range(chips):
            to_mate(b, d, source(b), me).wait_send()


def attention(query, keys, values, low, devices):
    rows, cols = query.shape
    chips = devices // 2
    dma = pltpu.SemaphoreType.DMA
    return pl.pallas_call(
        functools.partial(attention_kernel, devices),
        out_shape=jax.ShapeDtypeStruct((rows, cols), jnp.bfloat16),
        in_specs=[pl.BlockSpec(memory_space=pltpu.VMEM)] * 4,
        out_specs=pl.BlockSpec(memory_space=pltpu.VMEM),
        scratch_shapes=[
            pltpu.VMEM((devices * rows, cols), jnp.bfloat16),
            pltpu.VMEM((devices * rows, cols), jnp.bfloat16),
            pltpu.VMEM((cols // HS, rows, 1), jnp.float32),
            pltpu.VMEM((cols // HS, rows, 1), jnp.float32),
            pltpu.VMEM((rows, cols), jnp.float32),
            dma((4,)), dma((4, chips)), dma((4, chips)), dma((4, chips)), dma((4, chips)),
        ],
        compiler_params=pltpu.CompilerParams(
            collective_id=1, has_side_effects=True, vmem_limit_bytes=48 * 1024 * 1024),
        name="attention",
    )(query, keys, values, low[:, None])


def project_kernel(planes, x_ref, sq_ref, w_ref, q_out, k_out, v_out, x_all, sq_all, w_all, total_ref,
                   w_sem, x_send, x_recv, sq_send, sq_recv):
    z = lax.axis_index("tp")
    rows, width = x_ref.shape
    half = width // 2
    others = [(z + s) % planes for s in range(1, planes)]
    greet([{"tp": t} for t in others])

    def x_slot(origin, side):
        return x_all.at[origin * 2 + side]

    def hop(origin, side, sent, target):
        place = x_slot(origin, side)
        return send(place, place, x_send.at[sent, side], x_recv.at[origin, side], {"tp": target})

    def first_hop(side, sent, target):
        src = x_ref.at[:, pl.ds(side * half, half)]
        return send(src, x_slot(z, side), x_send.at[sent, side], x_recv.at[z, side], {"tp": target})

    def sq_copy(src, origin, target):
        return send(src, sq_all.at[origin], sq_send.at[target], sq_recv.at[origin], {"tp": target})

    def weights(origin):
        rows_of = pl.ds(pl.multiple_of(origin * width, width), width)
        return pltpu.make_async_copy(w_ref.at[:, rows_of, :], w_all.at[:, rows_of, :], w_sem.at[origin])

    for t in others:
        sq_copy(sq_ref, z, t).start()
    for side in range(2):

        @pl.when(z + 1 < planes)
        def _():
            first_hop(side, planes, z + 1).start()

        @pl.when(z > 0)
        def _():
            first_hop(side, planes + 1, z - 1).start()

    for s in range(planes):
        weights((z + s) % planes).start()
    total_ref[...] = jnp.zeros(total_ref.shape, jnp.float32)

    def multiply(block, origin, side):
        rows_of = pl.ds(pl.multiple_of(origin * width + side * half, half), half)

        def one(j, unused):
            total_ref[j] = total_ref[j] + jnp.dot(
                block[...], w_all[j, rows_of, :], preferred_element_type=jnp.float32)
            return unused

        lax.fori_loop(0, 3, one, 0)

    for s in range(planes):
        weights((z + s) % planes).wait()
    for side in range(2):
        multiply(x_ref.at[:, pl.ds(side * half, half)], z, side)
    for s in range(1, planes):
        for side in range(2):

            @pl.when(z - s >= 0)
            def _():
                hop(z - s, side, z - s, z).wait_recv()

                @pl.when(z + 1 < planes)
                def _():
                    hop(z - s, side, z - s, z + 1).start()

            @pl.when(z + s < planes)
            def _():
                hop(z + s, side, z + s, z).wait_recv()

                @pl.when(z > 0)
                def _():
                    hop(z + s, side, z + s, z - 1).start()

            @pl.when(z - s >= 0)
            def _():
                multiply(x_slot(z - s, side), z - s, side)

            @pl.when(z + s < planes)
            def _():
                multiply(x_slot(z + s, side), z + s, side)

    squares = sq_ref[0:1, :]
    for t in others:
        sq_copy(sq_all.at[t], t, t).wait_recv()
        squares = squares + sq_all[t][0:1, :]
    across = lax.broadcasted_iota(jnp.int32, (rows, rows), 0) == lax.broadcasted_iota(jnp.int32, (rows, rows), 1)
    column = jnp.sum(jnp.where(across, jnp.broadcast_to(squares, (rows, rows)), 0.0), axis=1, keepdims=True)
    scale = lax.rsqrt(column / D + eps)
    for j, out in enumerate((q_out, k_out, v_out)):
        out[...] = (total_ref[j] * scale).astype(out.dtype)
    for t in others:
        sq_copy(sq_ref, z, t).wait_send()
    for side in range(2):

        @pl.when(z + 1 < planes)
        def _():
            first_hop(side, planes, z + 1).wait_send()

        @pl.when(z > 0)
        def _():
            first_hop(side, planes + 1, z - 1).wait_send()

        for s in range(1, planes):

            @pl.when((z - s >= 0) & (z + 1 < planes))
            def _():
                hop(z - s, side, z - s, z + 1).wait_send()

            @pl.when((z + s < planes) & (z > 0))
            def _():
                hop(z + s, side, z + s, z - 1).wait_send()


def project(scaled, squares, weight, planes):
    rows, width = scaled.shape
    cols = weight.shape[2]
    dma = pltpu.SemaphoreType.DMA
    vmem = pl.BlockSpec(memory_space=pltpu.VMEM)
    result = jax.ShapeDtypeStruct((rows, cols), jnp.bfloat16)
    return pl.pallas_call(
        functools.partial(project_kernel, planes),
        out_shape=(result,) * 3,
        in_specs=[vmem, vmem, pl.BlockSpec(memory_space=pl.ANY)],
        out_specs=[vmem] * 3,
        scratch_shapes=[
            pltpu.VMEM((planes * 2, rows, width // 2), jnp.bfloat16),
            pltpu.VMEM((planes, 8, rows), jnp.float32),
            pltpu.VMEM(weight.shape, weight.dtype),
            pltpu.VMEM((3, rows, cols), jnp.float32),
            dma((planes,)), dma((planes + 2, 2)), dma((planes, 2)), dma((planes,)), dma((planes,)),
        ],
        compiler_params=pltpu.CompilerParams(
            collective_id=3, has_side_effects=True, vmem_limit_bytes=48 * 1024 * 1024),
        name="project",
    )(scaled, jnp.broadcast_to(squares[None, :], (8, rows)), weight)


def shifted(value, axis, by):
    devices = lax.axis_size(axis)
    pairs = [(i, i + by) for i in range(devices) if 0 <= i + by < devices]
    return lax.ppermute(value, axis, pairs)


def body(
    residual_in,
    features,
    filter_taps,
    filter_decay,
    skip_gain,
    out_weight,
    norm_gain,
    qkv_weight,
    doc_lengths,
):
    rows = residual_in.shape[0]
    local_width = residual_in.shape[1]
    channels = filter_taps.shape[0]
    span = filter_taps.shape[1]
    query_h = features[0]
    key_h = features[1]
    value_h = features[2]
    edge_keys, edge_values = shifted(
        (key_h[rows - (span - 1) :], value_h[rows - (span - 1) :]), "ctx", 1
    )
    mixed_in = key_h.astype(jnp.float32) * value_h.astype(jnp.float32)
    before = edge_keys.astype(jnp.float32) * edge_values.astype(jnp.float32)
    extended = jnp.concatenate([before, mixed_in], axis=0)
    tap_index = jnp.arange(span, dtype=jnp.float32)
    filt = filter_taps * jnp.exp(-filter_decay[:, None] * tap_index[None, :])
    kernel = filt[:, ::-1].T[:, None, :]
    conv = lax.conv_general_dilated(
        extended[None],
        kernel,
        (1,),
        [(0, 0)],
        dimension_numbers=("NHC", "HIO", "NHC"),
        feature_group_count=channels,
        precision=lax.Precision.HIGHEST,
    )[0]
    gated = (query_h.astype(jnp.float32) * (conv + skip_gain[None, :] * mixed_in)).astype(
        jnp.bfloat16
    )
    offset = lax.axis_index("tp") * local_width
    gain_local = lax.dynamic_slice_in_dim(norm_gain, offset, local_width, 0)
    parts = lax.axis_size("ctx")
    gated_all, columns = deal(gated, out_weight, parts, lax.axis_size("tp"))
    stream = residual_in.astype(jnp.float32) + jnp.dot(gated_all, columns, preferred_element_type=jnp.float32)
    mixed_stream = stream.astype(jnp.bfloat16)
    scaled = (stream * gain_local[None, :]).astype(jnp.bfloat16)
    squares = jnp.sum(stream * stream, axis=1)
    query, keys, values = project(scaled, squares, qkv_weight, lax.axis_size("tp"))
    ends = jnp.cumsum(doc_lengths)
    first = lax.axis_index("ctx") * rows
    q_pos = first + jnp.arange(rows, dtype=jnp.int32)
    low = jnp.max(jnp.where(ends[None, :] <= q_pos[:, None], ends[None, :], 0), axis=1).astype(jnp.int32)
    attended = attention(query, keys, values, low, parts)
    return (mixed_stream, attended)


def solution(mesh):
    return jax.shard_map(
        body,
        mesh=mesh,
        in_specs=(
            P("ctx", "tp"),
            P(None, "ctx", "tp"),
            P("tp", None),
            P("tp"),
            P("tp"),
            P("tp", None),
            P(),
            P(None, None, "tp"),
            P(),
        ),
        out_specs=(P("ctx", "tp"), P("ctx", "tp")),
        check_vma=False,
    )
```

```python
import functools
import jax
import jax.numpy as jnp
from jax import lax
from jax.experimental import pallas as pl
from jax.experimental.pallas import tpu as pltpu
from jax.sharding import PartitionSpec as P

D = 4096
HS = 128
LOG2E = 1.4426950408889634


eps = 1e-06


def flip(place, by):
    out = place
    bit = 1
    while bit <= by:
        if by & bit:
            out = out + bit - 2 * bit * ((place // bit) % 2)
        bit *= 2
    return out


def send(src, dst, sent, landed, device):
    return pltpu.make_async_remote_copy(
        src_ref=src, dst_ref=dst, send_sem=sent, recv_sem=landed,
        device_id=device, device_id_type=pl.DeviceIdType.MESH)


def greet(others):
    barrier = pltpu.get_barrier_semaphore()
    for other in others:
        pl.semaphore_signal(barrier, inc=1, device_id=other, device_id_type=pl.DeviceIdType.MESH)
    pl.semaphore_wait(barrier, len(others))


def deal_kernel(devices, planes, g_ref, w_ref, g_out, w_out, own_sem, g_send, g_recv, z_send, z_recv, p_send, p_recv, m_send, m_recv):
    me = lax.axis_index("ctx")
    z = lax.axis_index("tp")
    chips = devices // 2
    tokens, wide = g_ref.shape
    depth = w_ref.shape[0]
    width = w_out.shape[1]
    rows, half = depth // chips, width // 2
    chip = me // 2
    core = me % 2
    mate = chip * 2 + 1 - core
    partners = [flip(chip, d) * 2 + core for d in range(1, chips)]
    others = [(z + s) % planes for s in range(1, planes)]
    greet([{"ctx": p} for p in partners] + [{"ctx": mate}] + [{"tp": t} for t in others])

    def slot(origin, from_chip, from_core):
        return w_out.at[
            pl.ds(pl.multiple_of(origin * depth + from_chip * rows, rows), rows),
            pl.ds(pl.multiple_of(from_core * half, half), half)]

    part = wide // 2

    def g_slot(origin, side):
        return g_out.at[:, pl.ds(pl.multiple_of(origin * wide + side * part, part), part)]

    def to_plane(target):
        src = w_ref.at[
            pl.ds(pl.multiple_of(chip * rows, rows), rows),
            pl.ds(pl.multiple_of(target * width + core * half, half), half)]
        return send(src, slot(z, chip, core), z_send.at[target], z_recv.at[z], {"tp": target})

    def from_plane(origin):
        place = slot(origin, chip, core)
        return send(place, place, z_send.at[origin], z_recv.at[origin], {"tp": origin})

    def to_partner(s, d, from_chip, target):
        place = slot(others[s], from_chip, core)
        return send(place, place, p_send.at[s, d], p_recv.at[s, d], {"ctx": target})

    def to_mate(s, d, from_core):
        place = slot(others[s], flip(chip, d), from_core)
        return send(place, place, m_send.at[s, d], m_recv.at[s, d], {"ctx": mate})

    def hop(origin, side, sent, target):
        place = g_slot(origin, side)
        return send(place, place, g_send.at[sent, side], g_recv.at[origin, side], {"tp": target})

    def first_hop(side, sent, target):
        src = g_ref.at[:, pl.ds(side * part, part)]
        return send(src, g_slot(z, side), g_send.at[sent, side], g_recv.at[z, side], {"tp": target})

    for s in range(planes - 1):
        to_plane(others[s]).start()

    for side in range(2):

        @pl.when(z + 1 < planes)
        def _():
            first_hop(side, planes, z + 1).start()

        @pl.when(z > 0)
        def _():
            first_hop(side, planes + 1, z - 1).start()

    own = pltpu.make_async_copy(
        g_ref, g_out.at[:, pl.ds(pl.multiple_of(z * wide, wide), wide)], own_sem.at[0])
    own.start()
    kept = pltpu.make_async_copy(
        w_ref.at[:, pl.ds(pl.multiple_of(z * width, width), width)],
        w_out.at[pl.ds(pl.multiple_of(z * depth, depth), depth), :], own_sem.at[1])
    kept.start()

    def relay(s, side):
        @pl.when(z - s >= 0)
        def _():
            hop(z - s, side, z - s, z).wait_recv()

            @pl.when(z + 1 < planes)
            def _():
                hop(z - s, side, z - s, z + 1).start()

        @pl.when(z + s < planes)
        def _():
            hop(z + s, side, z + s, z).wait_recv()

            @pl.when(z > 0)
            def _():
                hop(z + s, side, z + s, z - 1).start()

    relayed = chips == 4
    direct = (1, 2) if relayed else tuple(range(1, chips))
    for s in range(planes - 1):
        from_plane(others[s]).wait_recv()
        for d in direct:
            to_partner(s, d, chip, partners[d - 1]).start()
        to_mate(s, 0, core).start()
    for side in range(2):
        relay(1, side)
    for s in range(planes - 1):
        for d in direct:
            to_partner(s, d, flip(chip, d), partners[d - 1]).wait_recv()
            to_mate(s, d, core).start()
            if relayed:

                @pl.when(core == d - 1)
                def _():
                    to_partner(s, 3, flip(chip, d), partners[2 - d]).start()
    for s in range(2, planes):
        for side in range(2):
            relay(s, side)
    for s in range(planes - 1):
        if relayed:
            to_partner(s, 3, flip(chip, 3), partners[2]).wait_recv()
            to_mate(s, 3, core).start()
    for s in range(planes - 1):
        to_plane(others[s]).wait_send()
        for d in range(1, chips):
            to_partner(s, d, flip(chip, d), partners[d - 1]).wait_send()
        for d in range(chips):
            to_mate(s, d, core).wait_send()
            to_mate(s, d, 1 - core).wait_recv()

    for side in range(2):

        @pl.when(z + 1 < planes)
        def _():
            first_hop(side, planes, z + 1).wait_send()

        @pl.when(z > 0)
        def _():
            first_hop(side, planes + 1, z - 1).wait_send()

    for s in range(1, planes):
        for side in range(2):

            @pl.when((z - s >= 0) & (z + 1 < planes))
            def _():
                hop(z - s, side, z - s, z + 1).wait_send()

            @pl.when((z + s < planes) & (z > 0))
            def _():
                hop(z + s, side, z + s, z - 1).wait_send()

    own.wait()
    kept.wait()


def deal(gated, out_weight, devices, planes):
    tokens, wide = gated.shape
    depth, full = out_weight.shape
    chips = devices // 2
    dma = pltpu.SemaphoreType.DMA
    return pl.pallas_call(
        functools.partial(deal_kernel, devices, planes),
        out_shape=(
            jax.ShapeDtypeStruct((tokens, planes * wide), gated.dtype),
            jax.ShapeDtypeStruct((planes * depth, full // planes), out_weight.dtype),
        ),
        in_specs=[pl.BlockSpec(memory_space=pl.ANY)] * 2,
        out_specs=[pl.BlockSpec(memory_space=pl.ANY)] * 2,
        scratch_shapes=[
            dma((2,)), dma((planes + 2, 2)), dma((planes, 2)), dma((planes,)), dma((planes,)),
            dma((planes - 1, chips)), dma((planes - 1, chips)), dma((planes - 1, chips)), dma((planes - 1, chips)),
        ],
        compiler_params=pltpu.CompilerParams(collective_id=2, has_side_effects=True),
        name="deal_gated_and_columns",
    )(gated, out_weight)


def attention_kernel(devices, q_ref, k_ref, v_ref, low_ref, out_ref, k_all, v_all, top_ref, total_ref, accum_ref,
                     own_sem, send_sem, recv_sem, mate_send, mate_recv):
    me = lax.axis_index("ctx")
    chips = devices // 2
    rows, cols = q_ref.shape
    chip = me // 2
    core = me % 2
    mate = chip * 2 + 1 - core
    partners = [flip(chip, d) * 2 + core for d in range(1, chips)]
    greet([{"ctx": p} for p in partners] + [{"ctx": mate}])
    outs = (k_all, v_all)
    ins = (k_ref, v_ref)
    part = rows // 2
    heads = cols // HS

    def slot(b, place):
        return outs[b % 2].at[pl.ds(pl.multiple_of(place * rows + (b // 2) * part, part), part), :]

    def source(b):
        return ins[b % 2].at[pl.ds((b // 2) * part, part), :]

    def to_partner(b, d, src, place, target):
        return send(src, slot(b, place), send_sem.at[b, d], recv_sem.at[b, d], {"ctx": target})

    def to_mate(b, d, src, place):
        return send(src, slot(b, place), mate_send.at[b, d], mate_recv.at[b, d], {"ctx": mate})

    def attend(place, side, causal):
        start = pl.multiple_of(place * rows + side * part, part)
        column = lax.broadcasted_iota(jnp.int32, (rows, part), 1) + start
        allowed = column >= low_ref[...]
        if causal:
            row = lax.broadcasted_iota(jnp.int32, (rows, part), 0) + me * rows
            allowed = allowed & (column <= row)
        lanes = [pl.ds(h * HS, HS) for h in range(heads)]
        tops = [top_ref[h] for h in range(heads)]
        totals = [total_ref[h] for h in range(heads)]
        sums = [accum_ref[:, lanes[h]] for h in range(heads)]
        for h in range(heads):
            scores = lax.dot_general(
                q_ref[:, lanes[h]], k_all[pl.ds(start, part), lanes[h]], (((1,), (1,)), ((), ())),
                preferred_element_type=jnp.float32)
            masked = jnp.where(allowed, scores * (HS ** (-0.5) * LOG2E), -1e30)
            new_top = jnp.maximum(tops[h], jnp.max(masked, axis=1, keepdims=True))
            factor = jnp.exp2(tops[h] - new_top)
            weights = jnp.exp2(masked - new_top)
            totals[h] = totals[h] * factor + jnp.sum(weights, axis=1, keepdims=True)
            sums[h] = sums[h] * factor + jnp.dot(
                weights.astype(jnp.bfloat16), v_all[pl.ds(start, part), lanes[h]],
                preferred_element_type=jnp.float32)
            tops[h] = new_top
        for h in range(heads):
            top_ref[h] = tops[h]
            total_ref[h] = totals[h]
            accum_ref[:, lanes[h]] = sums[h]

    def attend_earlier(place, side):
        @pl.when(place < me)
        def _():
            attend(place, side, False)

    for b in range(4):
        for d in ((1, 2) if chips == 4 else tuple(range(1, chips))):
            to_partner(b, d, source(b), me, partners[d - 1]).start()
        to_mate(b, 0, source(b), me).start()
        pltpu.make_async_copy(source(b), slot(b, me), own_sem.at[b]).start()
    top_ref[...] = jnp.full(top_ref.shape, -1e20, jnp.float32)
    total_ref[...] = jnp.zeros(total_ref.shape, jnp.float32)
    accum_ref[...] = jnp.zeros(accum_ref.shape, jnp.float32)

    def mate_landed(d, side):
        for b in (2 * side, 2 * side + 1):
            place = flip(chip, d) * 2 + 1 - core
            to_mate(b, d, slot(b, place), place).wait_recv()

    def partner_landed(d, side):
        for b in (2 * side, 2 * side + 1):
            place = partners[d - 1]
            to_partner(b, d, slot(b, place), place, place).wait_recv()
            to_mate(b, d, slot(b, place), place).start()
            if chips == 4 and d < 3:

                @pl.when(core == d - 1)
                def _():
                    to_partner(b, 3, slot(b, place), place, partners[2 - d]).start()

    for b in range(4):
        pltpu.make_async_copy(source(b), slot(b, me), own_sem.at[b]).wait()

    def own(side, unused):
        attend(me, side, True)
        return unused

    lax.fori_loop(0, 2, own, 0)
    for side in range(2):
        mate_landed(0, side)

    def beside(side, unused):
        attend_earlier(mate, side)
        return unused

    lax.fori_loop(0, 2, beside, 0)
    if chips == 4:
        for side in range(2):
            for d in (1, 2):
                partner_landed(d, side)
            for d in (1, 2):
                mate_landed(d, side)

            def near(i, unused):
                from_chip = (1 - i // 2) * flip(chip, 1) + (i // 2) * flip(chip, 2)
                attend_earlier(from_chip * 2 + i % 2, side)
                return unused

            lax.fori_loop(0, 4, near, 0)
        for side in range(2):
            partner_landed(3, side)
            mate_landed(3, side)

            def far(i, unused):
                attend_earlier(flip(chip, 3) * 2 + i, side)
                return unused

            lax.fori_loop(0, 2, far, 0)
    else:
        for side in range(2):
            for d in range(1, chips):
                partner_landed(d, side)
            for d in range(1, chips):
                mate_landed(d, side)

            def later(i, unused):
                attend_earlier(((chip + i // 2) % chips) * 2 + i % 2, side)
                return unused

            lax.fori_loop(2, 2 * chips, later, 0)
    for h in range(heads):
        lanes = pl.ds(h * HS, HS)
        out_ref[:, lanes] = (accum_ref[:, lanes] / total_ref[h]).astype(out_ref.dtype)
    for b in range(4):
        for d in range(1, chips):
            to_partner(b, d, source(b), me, partners[d - 1]).wait_send()
        for d in range(chips):
            to_mate(b, d, source(b), me).wait_send()


def attention(query, keys, values, low, devices):
    rows, cols = query.shape
    chips = devices // 2
    dma = pltpu.SemaphoreType.DMA
    return pl.pallas_call(
        functools.partial(attention_kernel, devices),
        out_shape=jax.ShapeDtypeStruct((rows, cols), jnp.bfloat16),
        in_specs=[pl.BlockSpec(memory_space=pltpu.VMEM)] * 4,
        out_specs=pl.BlockSpec(memory_space=pltpu.VMEM),
        scratch_shapes=[
            pltpu.VMEM((devices * rows, cols), jnp.bfloat16),
            pltpu.VMEM((devices * rows, cols), jnp.bfloat16),
            pltpu.VMEM((cols // HS, rows, 1), jnp.float32),
            pltpu.VMEM((cols // HS, rows, 1), jnp.float32),
            pltpu.VMEM((rows, cols), jnp.float32),
            dma((4,)), dma((4, chips)), dma((4, chips)), dma((4, chips)), dma((4, chips)),
        ],
        compiler_params=pltpu.CompilerParams(
            collective_id=1, has_side_effects=True, vmem_limit_bytes=48 * 1024 * 1024),
        name="attention",
    )(query, keys, values, low[:, None])


def project_kernel(planes, x_ref, sq_ref, w_ref, q_out, k_out, v_out, x_all, sq_all, w_all, total_ref,
                   w_sem, x_send, x_recv, sq_send, sq_recv):
    z = lax.axis_index("tp")
    rows, width = x_ref.shape
    half = width // 2
    others = [(z + s) % planes for s in range(1, planes)]
    greet([{"tp": t} for t in others])

    def x_slot(origin, side):
        return x_all.at[origin * 2 + side]

    def hop(origin, side, sent, target):
        place = x_slot(origin, side)
        return send(place, place, x_send.at[sent, side], x_recv.at[origin, side], {"tp": target})

    def first_hop(side, sent, target):
        src = x_ref.at[:, pl.ds(side * half, half)]
        return send(src, x_slot(z, side), x_send.at[sent, side], x_recv.at[z, side], {"tp": target})

    def sq_copy(src, origin, target):
        return send(src, sq_all.at[origin], sq_send.at[target], sq_recv.at[origin], {"tp": target})

    def weights(origin):
        rows_of = pl.ds(pl.multiple_of(origin * width, width), width)
        return pltpu.make_async_copy(w_ref.at[:, rows_of, :], w_all.at[:, rows_of, :], w_sem.at[origin])

    for t in others:
        sq_copy(sq_ref, z, t).start()
    for side in range(2):

        @pl.when(z + 1 < planes)
        def _():
            first_hop(side, planes, z + 1).start()

        @pl.when(z > 0)
        def _():
            first_hop(side, planes + 1, z - 1).start()

    for s in range(planes):
        weights((z + s) % planes).start()
    total_ref[...] = jnp.zeros(total_ref.shape, jnp.float32)

    def multiply(block, origin, side):
        rows_of = pl.ds(pl.multiple_of(origin * width + side * half, half), half)

        def one(j, unused):
            total_ref[j] = total_ref[j] + jnp.dot(
                block[...], w_all[j, rows_of, :], preferred_element_type=jnp.float32)
            return unused

        lax.fori_loop(0, 3, one, 0)

    for s in range(planes):
        weights((z + s) % planes).wait()
    for side in range(2):
        multiply(x_ref.at[:, pl.ds(side * half, half)], z, side)
    for s in range(1, planes):
        for side in range(2):

            @pl.when(z - s >= 0)
            def _():
                hop(z - s, side, z - s, z).wait_recv()

                @pl.when(z + 1 < planes)
                def _():
                    hop(z - s, side, z - s, z + 1).start()

            @pl.when(z + s < planes)
            def _():
                hop(z + s, side, z + s, z).wait_recv()

                @pl.when(z > 0)
                def _():
                    hop(z + s, side, z + s, z - 1).start()

            @pl.when(z - s >= 0)
            def _():
                multiply(x_slot(z - s, side), z - s, side)

            @pl.when(z + s < planes)
            def _():
                multiply(x_slot(z + s, side), z + s, side)

    squares = sq_ref[0:1, :]
    for t in others:
        sq_copy(sq_all.at[t], t, t).wait_recv()
        squares = squares + sq_all[t][0:1, :]
    across = lax.broadcasted_iota(jnp.int32, (rows, rows), 0) == lax.broadcasted_iota(jnp.int32, (rows, rows), 1)
    column = jnp.sum(jnp.where(across, jnp.broadcast_to(squares, (rows, rows)), 0.0), axis=1, keepdims=True)
    scale = lax.rsqrt(column / D + eps)
    for j, out in enumerate((q_out, k_out, v_out)):
        out[...] = (total_ref[j] * scale).astype(out.dtype)
    for t in others:
        sq_copy(sq_ref, z, t).wait_send()
    for side in range(2):

        @pl.when(z + 1 < planes)
        def _():
            first_hop(side, planes, z + 1).wait_send()

        @pl.when(z > 0)
        def _():
            first_hop(side, planes + 1, z - 1).wait_send()

        for s in range(1, planes):

            @pl.when((z - s >= 0) & (z + 1 < planes))
            def _():
                hop(z - s, side, z - s, z + 1).wait_send()

            @pl.when((z + s < planes) & (z > 0))
            def _():
                hop(z + s, side, z + s, z - 1).wait_send()


def project(scaled, squares, weight, planes):
    rows, width = scaled.shape
    cols = weight.shape[2]
    dma = pltpu.SemaphoreType.DMA
    vmem = pl.BlockSpec(memory_space=pltpu.VMEM)
    result = jax.ShapeDtypeStruct((rows, cols), jnp.bfloat16)
    return pl.pallas_call(
        functools.partial(project_kernel, planes),
        out_shape=(result,) * 3,
        in_specs=[vmem, vmem, pl.BlockSpec(memory_space=pl.ANY)],
        out_specs=[vmem] * 3,
        scratch_shapes=[
            pltpu.VMEM((planes * 2, rows, width // 2), jnp.bfloat16),
            pltpu.VMEM((planes, 8, rows), jnp.float32),
            pltpu.VMEM(weight.shape, weight.dtype),
            pltpu.VMEM((3, rows, cols), jnp.float32),
            dma((planes,)), dma((planes + 2, 2)), dma((planes, 2)), dma((planes,)), dma((planes,)),
        ],
        compiler_params=pltpu.CompilerParams(
            collective_id=3, has_side_effects=True, vmem_limit_bytes=48 * 1024 * 1024),
        name="project",
    )(scaled, jnp.broadcast_to(squares[None, :], (8, rows)), weight)


def shifted(value, axis, by):
    devices = lax.axis_size(axis)
    pairs = [(i, i + by) for i in range(devices) if 0 <= i + by < devices]
    return lax.ppermute(value, axis, pairs)


def body(
    residual_in,
    features,
    filter_taps,
    filter_decay,
    skip_gain,
    out_weight,
    norm_gain,
    qkv_weight,
    doc_lengths,
):
    rows = residual_in.shape[0]
    local_width = residual_in.shape[1]
    channels = filter_taps.shape[0]
    span = filter_taps.shape[1]
    query_h = features[0]
    key_h = features[1]
    value_h = features[2]
    edge_keys, edge_values = shifted(features[1:, rows - (span - 1) :], "ctx", 1)
    mixed_in = key_h.astype(jnp.float32) * value_h.astype(jnp.float32)
    before = edge_keys.astype(jnp.float32) * edge_values.astype(jnp.float32)
    extended = jnp.concatenate([before, mixed_in], axis=0)
    tap_index = jnp.arange(span, dtype=jnp.float32)
    filt = filter_taps * jnp.exp(-filter_decay[:, None] * tap_index[None, :])
    kernel = filt[:, ::-1].T[:, None, :]
    conv = lax.conv_general_dilated(
        extended[None],
        kernel,
        (1,),
        [(0, 0)],
        dimension_numbers=("NHC", "HIO", "NHC"),
        feature_group_count=channels,
        precision=lax.Precision.HIGHEST,
    )[0]
    gated = (query_h.astype(jnp.float32) * (conv + skip_gain[None, :] * mixed_in)).astype(
        jnp.bfloat16
    )
    offset = lax.axis_index("tp") * local_width
    gain_local = lax.dynamic_slice_in_dim(norm_gain, offset, local_width, 0)
    parts = lax.axis_size("ctx")
    gated_all, columns = deal(gated, out_weight, parts, lax.axis_size("tp"))
    stream = residual_in.astype(jnp.float32) + jnp.dot(gated_all, columns, preferred_element_type=jnp.float32)
    mixed_stream = stream.astype(jnp.bfloat16)
    scaled = (stream * gain_local[None, :]).astype(jnp.bfloat16)
    squares = jnp.sum(stream * stream, axis=1)
    query, keys, values = project(scaled, squares, qkv_weight, lax.axis_size("tp"))
    ends = jnp.cumsum(doc_lengths)
    first = lax.axis_index("ctx") * rows
    q_pos = first + jnp.arange(rows, dtype=jnp.int32)
    low = jnp.max(jnp.where(ends[None, :] <= q_pos[:, None], ends[None, :], 0), axis=1).astype(jnp.int32)
    attended = attention(query, keys, values, low, parts)
    return (mixed_stream, attended)


def solution(mesh):
    return jax.shard_map(
        body,
        mesh=mesh,
        in_specs=(
            P("ctx", "tp"),
            P(None, "ctx", "tp"),
            P("tp", None),
            P("tp"),
            P("tp"),
            P("tp", None),
            P(),
            P(None, None, "tp"),
            P(),
        ),
        out_specs=(P("ctx", "tp"), P("ctx", "tp")),
        check_vma=False,
    )
```
